1024 devices in a mesh: dp: 128 (over z, y), grp: 8 (over x, core).
Axes of the slice: x: 4, y: 8, z: 16, core: 2. Of those that a mesh axis runs over, the one named last changes fastest.
Arguments:
- user_vec: bfloat16 [32768, 256], P('dp'), may hold values from -40 to 40
- item_emb: bfloat16 [32768, 256], P(('dp', 'grp')), may hold values from -40 to 40
- w_one: bfloat16 [256, 1024], replicated, may hold values from -0.375 to 0.375
- w_two: bfloat16 [1024, 256], replicated, may hold values from -0.1875 to 0.1875
- item_owner: int32 [32768, 2], P(('dp', 'grp')), may hold values from 0 to 7, all different within a row; in each aligned block of 32 rows (0 to 31, 32 to 63, ...) at most 16 rows name the same one
- item_slot: int32 [32768, 2], P(('dp', 'grp')), may hold values from 0 to 63
Outputs:
- table_grad: float32 [65536, 256], P(('dp', 'grp'))
- w_grads: float32 [1024, 512], P(('dp', 'grp'))
The draws below stay inside these ranges and needn't reach their ends.
Inputs may be any that keep to these rules, and one draw needn't show every extreme that they name: `item_owner`: the two owners of an item differ. Among the rows of one device each owner index is named by at most 16 rows, and by exactly 16 on some devices.
All inputs are finite; a program needn't handle non-finite values.
Results may differ from the reference program's by a relative error of at most 0.015.
Values may be sent and summed in bfloat16 or wider, within the bound.
No kernel may reach another device: no remote copies, remote signals or barrier semaphores. Data moves between devices by JAX's collectives and lax.ppermute only.
A program may use at most 32 MiB of HBM per device.

```python
import math
import jax
import jax.numpy as jnp
import numpy as np
from jax import lax

W = 256
EMB = 256
H = 1024
IDEV = 32
TOUCH = 64
UDP = 256
BATCH = 32768
ROWS = 65536
CAP = 16
N_DP = 128
N_GRP = 8


def row_scales(key, count):
    return jnp.exp(jax.random.uniform(key, (count, 1), jnp.float32, 0.0, 2.302585))


def draw_user_vec(key, part):
    key = jax.random.fold_in(key, 7)
    key_scale, key_base = jax.random.split(key, 2)
    scales = row_scales(key_scale, BATCH)
    base_vals = jnp.clip(jax.random.normal(key_base, (BATCH, W), jnp.float32), -4.0, 4.0)
    return (base_vals * scales).astype(jnp.bfloat16)


def draw_item_emb(key, part):
    key = jax.random.fold_in(key, 9)
    key_scale, key_base = jax.random.split(key, 2)
    scales = row_scales(key_scale, BATCH)
    base_vals = jnp.clip(jax.random.normal(key_base, (BATCH, EMB), jnp.float32), -4.0, 4.0)
    return (base_vals * scales).astype(jnp.bfloat16)


def set_ends(values, own_key, low, high):
    longest = values.shape.index(max(values.shape))
    spots = []
    for shift in (0, 1):
        where = [jax.random.randint(jax.random.fold_in(own_key, axis), (), 0, length) for axis, length in enumerate(values.shape)]
        where[longest] = (where[longest] + shift) % values.shape[longest]
        spots.append(tuple(where))
    return values.at[spots[0]].set(low).at[spots[1]].set(high)


def routed_block(stream_key, own, number, rows, count, top, most, lean):
    order = jax.random.permutation(stream_key, count)
    crowded, usual = load_shares(count, rows * top, most, lean, True), load_shares(count, rows * top, most, lean, False)
    places = jnp.arange(count)

    def named(tallies, offset_by):
        used = int((tallies > 0).sum())
        fixed = max(1, used // 4)
        shifted = fixed + (places - fixed + offset_by * (used - fixed)) % max(1, count - fixed)
        return jnp.zeros((count,), jnp.int32).at[order[jnp.where(places < fixed, places, shifted)]].set(jnp.asarray(tallies, jnp.int32))

    tallies = jnp.where(number % 4 == 0, named(crowded, number // 4), named(usual, number - number // 4 - 1))
    mixed = jax.random.permutation(jax.random.fold_in(own, 3), count)
    donor, taker = mixed[0:count // 2 * 2:2], mixed[1:count // 2 * 2:2]
    slack = jnp.minimum(tallies[donor] - 1, most - tallies[taker]) // 2
    slack = jnp.where((donor == order[0]) | (taker == order[0]) | (tallies[taker] == 0), 0, jnp.maximum(slack, 0))
    shifted = jax.random.randint(jax.random.fold_in(own, 4), (count // 2,), 0, 1 << 20) % (slack + 1)
    tallies = tallies.at[donor].add(-shifted).at[taker].add(shifted)
    members = jnp.searchsorted(jnp.cumsum(tallies), jnp.arange(rows * top), side="right").astype(jnp.int32)
    listing = members.reshape(top, rows).T
    listing = listing[jax.random.permutation(jax.random.fold_in(own, 1), rows)]
    offset_by = jax.random.randint(jax.random.fold_in(own, 2), (rows, 1), 0, top)
    return jnp.take_along_axis(listing, (jnp.arange(top)[None, :] + offset_by) % top, axis=1)


def load_shares(count, total, limit, slope, full):
    portions = [(1 << 20) // math.isqrt(grade ** slope) + 1 for grade in range(1, count + 1)]
    largest = limit if full else min(limit, max(-(-total // count), total * portions[0] // sum(portions)))
    least = 1 if total - largest >= count - 1 else 0
    given, spare = [largest] + [least] * (count - 1), total - largest - least * (count - 1)
    while spare > 0:
        candidates = [i for i in range(1, count) if given[i] < largest] or [i for i in range(1, count) if given[i] < limit]
        whole, budget = sum([portions[i] for i in candidates]), spare
        for i in candidates:
            more = min(limit - given[i], max(1, budget * portions[i] // whole), spare)
            given[i] = given[i] + more
            spare = spare - more
    return np.array(given)


def centred(own_key, extent, deviation, reach, kind=jnp.bfloat16):
    result = deviation * jax.random.normal(own_key, extent, jnp.float32)
    return jnp.clip(result, min=-reach, max=reach).astype(kind)


def setup_inputs(seed: int = 0) -> dict:
    seeds = jax.random.split(jax.random.key(seed), 7)
    user_vec = draw_user_vec(jax.random.fold_in(seeds[6], 71), 0)
    item_emb = draw_item_emb(jax.random.fold_in(seeds[6], 71), 0)
    w_one = centred(seeds[2], (EMB, H), EMB ** -0.5, 0.375)
    w_two = centred(seeds[3], (H, W), H ** -0.5, 0.1875)
    item_owner_keys = jax.random.split(jax.random.fold_in(seeds[4], 1), BATCH // IDEV)
    item_owner_turns = jax.random.permutation(jax.random.fold_in(seeds[4], 3), BATCH // IDEV)
    item_owner = jax.vmap(lambda own, number: routed_block(jax.random.fold_in(seeds[4], 2), own, number, IDEV, N_GRP, 2, CAP, 2))(item_owner_keys, item_owner_turns).reshape((BATCH, 2))
    item_slot = set_ends(jax.random.randint(seeds[5], (BATCH, 2), 0, TOUCH), jax.random.fold_in(seeds[5], 1), 0, TOUCH - 1).astype(jnp.int32)
    return {"user_vec": user_vec, "item_emb": item_emb, "w_one": w_one, "w_two": w_two, "item_owner": item_owner, "item_slot": item_slot}


sharpness_divisor = 0.02
epsilon = 1e-06

def unit_rows(values):
    return values * lax.rsqrt(lax.optimization_barrier(jnp.sum(values * values, axis=-1, keepdims=True)) + epsilon)

def silu_slope(preact):
    sigmoid = jax.nn.sigmoid(preact)
    return (preact * sigmoid, sigmoid * (1.0 + preact * (1.0 - sigmoid)))

def reference(user_vec, item_emb, w_one, w_two, item_owner, item_slot):
    query_unit_vectors = unit_rows(user_vec.astype(jnp.float32)).astype(jnp.bfloat16)
    preact = jnp.dot(item_emb, w_one, preferred_element_type=jnp.float32)
    hidden_f, slopes = silu_slope(preact)
    hidden = hidden_f.astype(jnp.bfloat16)
    item_out = jnp.dot(hidden, w_two, preferred_element_type=jnp.float32)
    item_scale = lax.rsqrt(lax.optimization_barrier(jnp.sum(item_out * item_out, axis=1, keepdims=True)) + epsilon)
    item_dir = item_out * item_scale
    candidate_unit_vectors = item_dir.astype(jnp.bfloat16)
    user_blocks = query_unit_vectors.reshape(N_DP, UDP, W)
    columns = jnp.arange(BATCH, dtype=jnp.int32)

    def add_block(running, inputs):
        query_block_height, block_index = inputs
        angle_similarity_scores = jnp.dot(query_block_height, candidate_unit_vectors.T, preferred_element_type=jnp.float32) / sharpness_divisor
        powers = jnp.exp(angle_similarity_scores)
        row_sums = lax.optimization_barrier(jnp.sum(powers, axis=1, keepdims=True))
        row_ids = block_index * UDP + jnp.arange(UDP, dtype=jnp.int32)
        target = (columns[None, :] == row_ids[:, None]).astype(jnp.float32)
        logit_cot = (powers / row_sums - target).astype(jnp.bfloat16)
        return (running + jnp.dot(logit_cot.T, query_block_height, preferred_element_type=jnp.float32), None)
    unit_cot, _ = lax.scan(add_block, jnp.zeros((BATCH, W), jnp.float32), (user_blocks, jnp.arange(N_DP, dtype=jnp.int32)))
    along = lax.optimization_barrier(jnp.sum(item_dir * unit_cot, axis=1, keepdims=True))
    out_cot = ((unit_cot - item_dir * along) * item_scale).astype(jnp.bfloat16)
    preact_cot = (jnp.dot(out_cot, w_two.T, preferred_element_type=jnp.float32) * slopes).astype(jnp.bfloat16)
    emb_cot = jnp.dot(preact_cot, w_one.T, preferred_element_type=jnp.float32)
    w_grads = jnp.concatenate([jnp.dot(preact_cot.T, item_emb, preferred_element_type=jnp.float32), jnp.dot(hidden.T, out_cot, preferred_element_type=jnp.float32)], axis=1)
    group_ids = jnp.arange(BATCH, dtype=jnp.int32) // UDP
    target_rows = (group_ids[:, None] * N_GRP + item_owner) * TOUCH + item_slot
    table_grad = jax.ops.segment_sum(jnp.concatenate([emb_cot, emb_cot], axis=0), jnp.concatenate([target_rows[:, 0], target_rows[:, 1]]).astype(jnp.int32), num_segments=ROWS)
    return (table_grad, w_grads)
```

```python
import jax
import jax.numpy as jnp
from jax import lax
from jax.experimental import pallas as pl
from jax.experimental.pallas import tpu as pltpu
from jax.sharding import Mesh, PartitionSpec as P

TOUCH = 64
NZ, NY, NX, NC = 16, 8, 4, 2
ITEMS = 32
EMB = 256
W = 256
H = 1024
GROUP = ITEMS * NX * NC
HALF = GROUP // NC
USERS = NY * GROUP
SCORE_BLOCK = 256
META = 128
FACT = EMB + W + META

inv_temperature = 1.0 / 0.02
epsilon = 1e-06
f32, bf16 = jnp.float32, jnp.bfloat16


def nn(left, right):
    return lax.dot_general(left, right, (((1,), (0,)), ((), ())), preferred_element_type=f32)


def nt(left, right):
    return lax.dot_general(left, right, (((1,), (1,)), ((), ())), preferred_element_type=f32)


def tn(left, right):
    return lax.dot_general(left, right, (((0,), (0,)), ((), ())), preferred_element_type=f32)


def unit_rows(values):
    return values * lax.rsqrt(jnp.sum(values * values, axis=-1, keepdims=True) + epsilon)


def call(body, outs, args, flops, grid=None, in_specs=None, out_specs=None, scratch=(), exps=0):
    moved = sum(a.size * a.dtype.itemsize for a in args)
    moved += sum(o.size * o.dtype.itemsize for o in outs)
    extra = {} if grid is None else dict(grid=grid, in_specs=in_specs, out_specs=out_specs)
    return pl.pallas_call(
        body,
        out_shape=outs,
        scratch_shapes=list(scratch),
        cost_estimate=pl.CostEstimate(flops=flops, bytes_accessed=moved, transcendentals=exps),
        compiler_params=pltpu.CompilerParams(vmem_limit_bytes=24 * 1024 * 1024),
        **extra,
    )(*args)


def shape(dims, kind):
    return jax.ShapeDtypeStruct(dims, kind)


def user_kernel(me_ref, user_hbm, spread_ref, positive_ref, half_ref, own_ref, sems):
    core = lax.rem(me_ref[0], NC)
    half = pl.ds(pl.multiple_of(core * HALF, HALF), HALF)
    own = pl.ds(pl.multiple_of(me_ref[0] * ITEMS, ITEMS), ITEMS)
    half_copy = pltpu.make_async_copy(user_hbm.at[half], half_ref, sems.at[0])
    own_copy = pltpu.make_async_copy(user_hbm.at[own], own_ref, sems.at[1])
    half_copy.start()
    own_copy.start()
    half_copy.wait()
    unit = unit_rows(half_ref[...].astype(f32)).astype(bf16)
    for peer in range(NY):
        spread_ref[peer] = unit
    own_copy.wait()
    positive_ref[...] = unit_rows(own_ref[...].astype(f32)).astype(bf16)


def tower_kernel(
    emb_ref, w_one_ref, w_two_ref, owner_ref, slot_ref, spread_ref, dir_ref, scale_ref, base_ref
):
    emb = emb_ref[...]
    pair = lax.broadcasted_iota(jnp.int32, (2, META), 0)
    lane = lax.broadcasted_iota(jnp.int32, (2, META), 1)
    at_owner = jnp.where(lane == 2 * pair, 1.0, 0.0)
    at_slot = jnp.where(lane == 2 * pair + 1, 1.0, 0.0)
    meta = tn(owner_ref[...].astype(f32), at_owner) + tn(slot_ref[...].astype(f32), at_slot)
    base_ref[:, :EMB] = emb
    base_ref[:, EMB:] = meta.astype(bf16)
    preact = nn(emb, w_one_ref[...])
    hidden = (preact * jax.nn.sigmoid(preact)).astype(bf16)
    item_out = nn(hidden, w_two_ref[...])
    scale = lax.rsqrt(jnp.sum(item_out * item_out, axis=1, keepdims=True) + epsilon)
    item_dir = item_out * scale
    unit = item_dir.astype(bf16)
    for peer in range(NZ):
        spread_ref[peer] = unit
    dir_ref[...] = item_dir
    scale_ref[...] = jnp.broadcast_to(scale, (ITEMS, 128))


def score_kernel(items_ref, own_ref, other_ref, powers_ref, spread_ref, sums_ref):
    items = items_ref[...]
    for step in range(USERS // SCORE_BLOCK):
        users_ref = own_ref if step < USERS // SCORE_BLOCK // 2 else other_ref
        first = step * SCORE_BLOCK % (USERS // 2)
        scores = nt(items, users_ref[first : first + SCORE_BLOCK, :]) * inv_temperature
        powers = jnp.exp(scores)
        first = step * SCORE_BLOCK
        powers_ref[:, first : first + SCORE_BLOCK] = powers.astype(bf16)
        sums = jnp.sum(powers, axis=0, keepdims=True)
        for k in range(SCORE_BLOCK // 128):
            row = first // 128 + k
            sums_ref[row : row + 1, :] = sums[:, k * 128 : (k + 1) * 128]
    spread_ref[...] = jnp.broadcast_to(sums_ref[...].astype(bf16)[None], spread_ref.shape)


def unit_cot_kernel(me_ref, parts_ref, own_ref, other_ref, powers_ref, out_ref, scaled_ref):
    half = USERS // 128 // 2
    core = lax.rem(me_ref[0], NC)
    mine = parts_ref[core].astype(f32)
    theirs = parts_ref[1 - core].astype(f32)
    for peer in range(1, NY * NX):
        mine += parts_ref[NC * peer + core].astype(f32)
        theirs += parts_ref[NC * peer + 1 - core].astype(f32)
    totals = mine + jnp.concatenate([theirs[half:], theirs[:half]], axis=0)
    inverse = jnp.transpose(1.0 / totals)
    for k in range(USERS // 128):
        users_ref = own_ref if k < half else other_ref
        first = k % half * 128
        block = users_ref[first : first + 128, :].astype(f32) * inverse[:, k : k + 1]
        scaled_ref[k * 128 : (k + 1) * 128, :] = block.astype(bf16)
    out_ref[...] = nn(powers_ref[...], scaled_ref[...]).astype(bf16)


def cot_kernel(parts_ref, positive_ref, dir_ref, scale_ref, base_ref, spread_ref):
    unit_cot = parts_ref[0].astype(f32)
    for peer in range(1, NZ):
        unit_cot += parts_ref[peer].astype(f32)
    unit_cot -= positive_ref[...].astype(f32)
    item_dir = dir_ref[...]
    along = jnp.sum(item_dir * unit_cot, axis=1, keepdims=True)
    out_cot = ((unit_cot - item_dir * along) * scale_ref[:, :1]).astype(bf16)
    base = base_ref[...]
    for peer in range(NX):
        spread_ref[peer, :, : EMB + META] = base
        spread_ref[peer, :, EMB + META :] = out_cot


def grads_kernel(me_ref, fact_ref, w_one_ref, w_two_ref, table_ref, part_ref):
    me = me_ref[0]
    emb = fact_ref[:, :EMB]
    meta = fact_ref[:, EMB : EMB + META].astype(f32)
    cot = fact_ref[:, EMB + META :]
    w_one = w_one_ref[...]
    preact = nn(emb, w_one)
    sig = jax.nn.sigmoid(preact)
    hidden = (preact * sig).astype(bf16)
    slopes = sig * (1.0 + preact * (1.0 - sig))
    preact_cot = (nt(cot, w_two_ref[...]) * slopes).astype(bf16)
    emb_cot = nt(preact_cot, w_one)
    mine = me.astype(f32)
    slots = lax.broadcasted_iota(jnp.int32, (GROUP, TOUCH), 1).astype(f32)
    placing = jnp.where((meta[:, 0:1] == mine) & (meta[:, 1:2] == slots), 1.0, 0.0)
    placing += jnp.where((meta[:, 2:3] == mine) & (meta[:, 3:4] == slots), 1.0, 0.0)
    table_ref[...] = tn(placing.astype(bf16), emb_cot.astype(bf16))
    count = H // (NX * NC)
    unit = lax.broadcasted_iota(jnp.int32, (H, count), 0)
    column = lax.broadcasted_iota(jnp.int32, (H, count), 1)
    pick = jnp.where(unit == column * (NX * NC) + me, 1.0, 0.0).astype(bf16)
    part_ref[:, 0, :] = tn(nn(preact_cot, pick).astype(bf16), emb).astype(bf16)
    part_ref[:, 1, :] = tn(nn(hidden, pick).astype(bf16), cot).astype(bf16)


def gather_pair(values):
    return lax.all_gather(values, "c", axis=0, tiled=True)


def trade_pair(values):
    return lax.ppermute(values, "c", [(0, 1), (1, 0)])


def on_device(user_vec, item_emb, w_one, w_two, item_owner, item_slot):
    me = lax.axis_index("x") * NC + lax.axis_index("c")
    place = me.reshape(1)
    vmem = pl.BlockSpec(memory_space=pltpu.VMEM)
    smem = pl.BlockSpec(memory_space=pltpu.SMEM)
    hbm = pl.BlockSpec(memory_space=pltpu.HBM)
    user_spread, positive = call(
        user_kernel,
        (shape((NY, HALF, W), bf16), shape((ITEMS, W), bf16)),
        (place, user_vec),
        4 * HALF * W,
        grid=(),
        in_specs=[smem, hbm],
        out_specs=(vmem, vmem),
        scratch=(
            pltpu.VMEM((HALF, W), bf16),
            pltpu.VMEM((ITEMS, W), bf16),
            pltpu.SemaphoreType.DMA((2,)),
        ),
    )
    users = lax.all_to_all(user_spread, "y", 0, 0)
    users = users.reshape(NY * HALF, W)
    others = trade_pair(users)
    item_spread, item_dir, item_scale, base = call(
        tower_kernel,
        (
            shape((NZ, ITEMS, W), bf16),
            shape((ITEMS, W), f32),
            shape((ITEMS, 128), f32),
            shape((ITEMS, EMB + META), bf16),
        ),
        (item_emb, w_one, w_two, item_owner.T, item_slot.T),
        4 * ITEMS * EMB * H,
    )
    count = NZ * ITEMS
    items = lax.all_to_all(item_spread, "z", 0, 0).reshape(count, W)
    powers, sums = call(
        score_kernel,
        (shape((count, USERS), bf16), shape((NY * NX * NC, USERS // 128, 128), bf16)),
        (items, users, others),
        2 * count * USERS * W,
        scratch=(pltpu.VMEM((USERS // 128, 128), f32),),
        exps=count * USERS,
    )
    sums = lax.all_to_all(sums, ("y", "x", "c"), 0, 0)
    partial = call(
        unit_cot_kernel,
        (shape((count, W), bf16),),
        (place, sums, users, others, powers),
        2 * count * USERS * W,
        grid=(),
        in_specs=[smem, vmem, vmem, vmem, vmem],
        out_specs=(vmem,),
        scratch=(pltpu.VMEM((USERS, W), bf16),),
    )[0]
    parts = lax.all_to_all(partial.reshape(NZ, ITEMS, W), "z", 0, 0)
    facts = call(
        cot_kernel,
        (shape((NX, ITEMS, FACT), bf16),),
        (parts, positive, item_dir, item_scale, base),
        NZ * ITEMS * W,
    )[0]
    facts = gather_pair(lax.all_to_all(facts, "x", 0, 0).reshape(NX * ITEMS, FACT))
    table_grad, part = call(
        grads_kernel,
        (shape((TOUCH, EMB), f32), shape((H // (NX * NC), 2, W), bf16)),
        (place, facts, w_one, w_two),
        2 * GROUP * EMB * H * 5,
        grid=(),
        in_specs=[smem, vmem, vmem, vmem],
        out_specs=(vmem, vmem),
    )
    part = lax.all_to_all(part, ("z", "y"), 0, 0, tiled=True)
    w_grads = jnp.sum(part.astype(f32), axis=0).reshape(1, EMB + W)
    return (table_grad, w_grads)


def solution(mesh):
    fine = Mesh(mesh.devices.reshape(NZ, NY, NX, NC), ("z", "y", "x", "c"))
    dp, every = ("z", "y"), ("z", "y", "x", "c")
    placed = (P(dp, None), P(every, None), P(), P(), P(every, None), P(every, None))
    return jax.shard_map(
        on_device,
        mesh=fine,
        in_specs=placed,
        out_specs=(P(every, None), P(every, None)),
        check_vma=False,
    )
```

```python
import jax
import jax.numpy as jnp
from jax import lax
from jax.experimental import pallas as pl
from jax.experimental.pallas import tpu as pltpu
from jax.sharding import Mesh, PartitionSpec as P

TOUCH = 64
NZ, NY, NX, NC = 16, 8, 4, 2
ITEMS = 32
EMB = 256
W = 256
H = 1024
GROUP = ITEMS * NX * NC
HALF = GROUP // NC
USERS = NY * GROUP
SCORE_BLOCK = 256
LARGE = 63 * 1024 * 1024 + 512 * 1024
META = 128
FACT = EMB + W + META

inv_temperature = 1.0 / 0.02
epsilon = 1e-06
f32, bf16 = jnp.float32, jnp.bfloat16


def nn(left, right):
    return lax.dot_general(left, right, (((1,), (0,)), ((), ())), preferred_element_type=f32)


def nt(left, right):
    return lax.dot_general(left, right, (((1,), (1,)), ((), ())), preferred_element_type=f32)


def tn(left, right):
    return lax.dot_general(left, right, (((0,), (0,)), ((), ())), preferred_element_type=f32)


def unit_rows(values):
    return values * lax.rsqrt(jnp.sum(values * values, axis=-1, keepdims=True) + epsilon)


def call(body, outs, args, flops, grid=None, in_specs=None, out_specs=None, scratch=(), exps=0, vmem=24 * 1024 * 1024):
    moved = sum(a.size * a.dtype.itemsize for a in args)
    moved += sum(o.size * o.dtype.itemsize for o in outs)
    extra = {} if grid is None else dict(grid=grid, in_specs=in_specs, out_specs=out_specs)
    return pl.pallas_call(
        body,
        out_shape=outs,
        scratch_shapes=list(scratch),
        cost_estimate=pl.CostEstimate(flops=flops, bytes_accessed=moved, transcendentals=exps),
        compiler_params=pltpu.CompilerParams(vmem_limit_bytes=vmem),
        **extra,
    )(*args)


def shape(dims, kind):
    return jax.ShapeDtypeStruct(dims, kind)


def user_kernel(me_ref, user_hbm, spread_ref, positive_ref, half_ref, own_ref, sems):
    core = lax.rem(me_ref[0], NC)
    half = pl.ds(pl.multiple_of(core * HALF, HALF), HALF)
    own = pl.ds(pl.multiple_of(me_ref[0] * ITEMS, ITEMS), ITEMS)
    half_copy = pltpu.make_async_copy(user_hbm.at[half], half_ref, sems.at[0])
    own_copy = pltpu.make_async_copy(user_hbm.at[own], own_ref, sems.at[1])
    half_copy.start()
    own_copy.start()
    half_copy.wait()
    unit = unit_rows(half_ref[...].astype(f32)).astype(bf16)
    for peer in range(NY):
        spread_ref[peer] = unit
    own_copy.wait()
    positive_ref[...] = unit_rows(own_ref[...].astype(f32)).astype(bf16)


def tower_kernel(
    emb_ref, w_one_ref, w_two_ref, owner_ref, slot_ref, spread_ref, dir_ref, scale_ref, base_ref
):
    emb = emb_ref[...]
    pair = lax.broadcasted_iota(jnp.int32, (2, META), 0)
    lane = lax.broadcasted_iota(jnp.int32, (2, META), 1)
    at_owner = jnp.where(lane == 2 * pair, 1.0, 0.0)
    at_slot = jnp.where(lane == 2 * pair + 1, 1.0, 0.0)
    meta = tn(owner_ref[...].astype(f32), at_owner) + tn(slot_ref[...].astype(f32), at_slot)
    base_ref[:, :EMB] = emb
    base_ref[:, EMB:] = meta.astype(bf16)
    preact = nn(emb, w_one_ref[...])
    hidden = (preact * jax.nn.sigmoid(preact)).astype(bf16)
    item_out = nn(hidden, w_two_ref[...])
    scale = lax.rsqrt(jnp.sum(item_out * item_out, axis=1, keepdims=True) + epsilon)
    item_dir = item_out * scale
    unit = item_dir.astype(bf16)
    for peer in range(NZ):
        spread_ref[peer] = unit
    dir_ref[...] = item_dir
    scale_ref[...] = jnp.broadcast_to(scale, (ITEMS, 128))


def score_kernel(items_ref, own_ref, other_ref, powers_ref, sums_ref):
    items = items_ref[...]
    for step in range(USERS // SCORE_BLOCK):
        users_ref = own_ref if step < USERS // SCORE_BLOCK // 2 else other_ref
        first = step * SCORE_BLOCK % (USERS // 2)
        scores = nt(items, users_ref[first : first + SCORE_BLOCK, :]) * inv_temperature
        powers = jnp.exp(scores)
        first = step * SCORE_BLOCK
        powers_ref[:, first : first + SCORE_BLOCK] = powers.astype(bf16)
        sums = jnp.sum(powers, axis=0, keepdims=True)
        for k in range(SCORE_BLOCK // 128):
            row = first // 128 + k
            sums_ref[row : row + 1, :] = sums[:, k * 128 : (k + 1) * 128]


def pair_kernel(mine_ref, theirs_ref, spread_ref):
    half = USERS // 128 // 2
    theirs = theirs_ref[...]
    total = mine_ref[...] + jnp.concatenate([theirs[half:], theirs[:half]], axis=0)
    spread_ref[...] = jnp.broadcast_to(total.astype(bf16)[None], spread_ref.shape)


def unit_cot_kernel(parts_ref, own_ref, other_ref, powers_ref, out_ref, scaled_ref):
    half = USERS // 128 // 2
    totals = parts_ref[0].astype(f32)
    for peer in range(1, NY * NX):
        totals += parts_ref[peer].astype(f32)
    inverse = jnp.transpose(1.0 / totals)
    for k in range(USERS // 128):
        users_ref = own_ref if k < half else other_ref
        first = k % half * 128
        block = users_ref[first : first + 128, :].astype(f32) * inverse[:, k : k + 1]
        scaled_ref[k * 128 : (k + 1) * 128, :] = block.astype(bf16)
    out_ref[...] = nn(powers_ref[...], scaled_ref[...]).astype(bf16)


def cot_kernel(parts_ref, positive_ref, dir_ref, scale_ref, base_ref, spread_ref):
    unit_cot = parts_ref[0].astype(f32)
    for peer in range(1, NZ):
        unit_cot += parts_ref[peer].astype(f32)
    unit_cot -= positive_ref[...].astype(f32)
    item_dir = dir_ref[...]
    along = jnp.sum(item_dir * unit_cot, axis=1, keepdims=True)
    out_cot = ((unit_cot - item_dir * along) * scale_ref[:, :1]).astype(bf16)
    base = base_ref[...]
    for peer in range(NX):
        spread_ref[peer, :, : EMB + META] = base
        spread_ref[peer, :, EMB + META :] = out_cot


def grads_kernel(me_ref, fact_ref, w_one_ref, w_two_ref, table_ref, part_ref):
    me = me_ref[0]
    emb = fact_ref[:, :EMB]
    meta = fact_ref[:, EMB : EMB + META].astype(f32)
    cot = fact_ref[:, EMB + META :]
    w_one = w_one_ref[...]
    preact = nn(emb, w_one)
    sig = jax.nn.sigmoid(preact)
    hidden = (preact * sig).astype(bf16)
    slopes = sig * (1.0 + preact * (1.0 - sig))
    preact_cot = (nt(cot, w_two_ref[...]) * slopes).astype(bf16)
    emb_cot = nt(preact_cot, w_one)
    mine = me.astype(f32)
    slots = lax.broadcasted_iota(jnp.int32, (GROUP, TOUCH), 1).astype(f32)
    placing = jnp.where((meta[:, 0:1] == mine) & (meta[:, 1:2] == slots), 1.0, 0.0)
    placing += jnp.where((meta[:, 2:3] == mine) & (meta[:, 3:4] == slots), 1.0, 0.0)
    table_ref[...] = tn(placing.astype(bf16), emb_cot.astype(bf16))
    count = H // (NX * NC)
    unit = lax.broadcasted_iota(jnp.int32, (H, count), 0)
    column = lax.broadcasted_iota(jnp.int32, (H, count), 1)
    pick = jnp.where(unit == column * (NX * NC) + me, 1.0, 0.0).astype(bf16)
    part_ref[:, 0, :] = tn(nn(preact_cot, pick).astype(bf16), emb).astype(bf16)
    part_ref[:, 1, :] = tn(nn(hidden, pick).astype(bf16), cot).astype(bf16)


def gather_pair(values):
    return lax.all_gather(values, "c", axis=0, tiled=True)


def trade_pair(values):
    return lax.ppermute(values, "c", [(0, 1), (1, 0)])


def on_device(user_vec, item_emb, w_one, w_two, item_owner, item_slot):
    me = lax.axis_index("x") * NC + lax.axis_index("c")
    place = me.reshape(1)
    vmem = pl.BlockSpec(memory_space=pltpu.VMEM)
    smem = pl.BlockSpec(memory_space=pltpu.SMEM)
    hbm = pl.BlockSpec(memory_space=pltpu.HBM)
    user_spread, positive = call(
        user_kernel,
        (shape((NY, HALF, W), bf16), shape((ITEMS, W), bf16)),
        (place, user_vec),
        4 * HALF * W,
        grid=(),
        in_specs=[smem, hbm],
        out_specs=(vmem, vmem),
        scratch=(
            pltpu.VMEM((HALF, W), bf16),
            pltpu.VMEM((ITEMS, W), bf16),
            pltpu.SemaphoreType.DMA((2,)),
        ),
        vmem=LARGE,
    )
    users = lax.all_to_all(user_spread, "y", 0, 0)
    users = users.reshape(NY * HALF, W)
    others = trade_pair(users)
    item_spread, item_dir, item_scale, base = call(
        tower_kernel,
        (
            shape((NZ, ITEMS, W), bf16),
            shape((ITEMS, W), f32),
            shape((ITEMS, 128), f32),
            shape((ITEMS, EMB + META), bf16),
        ),
        (item_emb, w_one, w_two, item_owner.T, item_slot.T),
        4 * ITEMS * EMB * H,
    )
    count = NZ * ITEMS
    items = lax.all_to_all(item_spread, "z", 0, 0).reshape(count, W)
    powers, sums = call(
        score_kernel,
        (shape((count, USERS), bf16), shape((USERS // 128, 128), f32)),
        (items, users, others),
        2 * count * USERS * W,
        exps=count * USERS,
    )
    sums = call(
        pair_kernel,
        (shape((NY * NX, USERS // 128, 128), bf16),),
        (sums, trade_pair(sums)),
        USERS,
    )[0]
    sums = lax.all_to_all(sums, ("y", "x"), 0, 0)
    partial = call(
        unit_cot_kernel,
        (shape((count, W), bf16),),
        (sums, users, others, powers),
        2 * count * USERS * W,
        scratch=(pltpu.VMEM((USERS, W), bf16),),
    )[0]
    parts = lax.all_to_all(partial.reshape(NZ, ITEMS, W), "z", 0, 0)
    facts = call(
        cot_kernel,
        (shape((NX, ITEMS, FACT), bf16),),
        (parts, positive, item_dir, item_scale, base),
        NZ * ITEMS * W,
    )[0]
    facts = gather_pair(lax.all_to_all(facts, "x", 0, 0).reshape(NX * ITEMS, FACT))
    table_grad, part = call(
        grads_kernel,
        (shape((TOUCH, EMB), f32), shape((H // (NX * NC), 2, W), bf16)),
        (place, facts, w_one, w_two),
        2 * GROUP * EMB * H * 5,
        grid=(),
        in_specs=[smem, vmem, vmem, vmem],
        out_specs=(vmem, vmem),
    )
    part = lax.all_to_all(part, ("z", "y"), 0, 0, tiled=True)
    w_grads = jnp.sum(part.astype(f32), axis=0).reshape(1, EMB + W)
    return (table_grad, w_grads)


def solution(mesh):
    fine = Mesh(mesh.devices.reshape(NZ, NY, NX, NC), ("z", "y", "x", "c"))
    dp, every = ("z", "y"), ("z", "y", "x", "c")
    placed = (P(dp, None), P(every, None), P(), P(), P(every, None), P(every, None))
    return jax.shard_map(
        on_device,
        mesh=fine,
        in_specs=placed,
        out_specs=(P(every, None), P(every, None)),
        check_vma=False,
    )
```

```python
import jax
import jax.numpy as jnp
from jax import lax
from jax.experimental import pallas as pl
from jax.experimental.pallas import tpu as pltpu
from jax.sharding import Mesh, PartitionSpec as P

TOUCH = 64
NZ, NY, NX, NC = 16, 8, 4, 2
ITEMS = 32
EMB = 256
W = 256
H = 1024
GROUP = ITEMS * NX * NC
HALF = GROUP // NC
USERS = NY * GROUP
SCORE_BLOCK = 256
LARGE = 63 * 1024 * 1024 + 512 * 1024
META = 128
FACT = EMB + W + META

score_exponent = 1.4426950408889634 / 0.02
epsilon = 1e-06
f32, bf16 = jnp.float32, jnp.bfloat16


def nn(left, right):
    return lax.dot_general(left, right, (((1,), (0,)), ((), ())), preferred_element_type=f32)


def nt(left, right):
    return lax.dot_general(left, right, (((1,), (1,)), ((), ())), preferred_element_type=f32)


def tn(left, right):
    return lax.dot_general(left, right, (((0,), (0,)), ((), ())), preferred_element_type=f32)


def unit_rows(values):
    return values * lax.rsqrt(jnp.sum(values * values, axis=-1, keepdims=True) + epsilon)


def call(body, outs, args, flops, grid=None, in_specs=None, out_specs=None, scratch=(), exps=0, vmem=24 * 1024 * 1024):
    moved = sum(a.size * a.dtype.itemsize for a in args)
    moved += sum(o.size * o.dtype.itemsize for o in outs)
    extra = {} if grid is None else dict(grid=grid, in_specs=in_specs, out_specs=out_specs)
    return pl.pallas_call(
        body,
        out_shape=outs,
        scratch_shapes=list(scratch),
        cost_estimate=pl.CostEstimate(flops=flops, bytes_accessed=moved, transcendentals=exps),
        compiler_params=pltpu.CompilerParams(vmem_limit_bytes=vmem),
        **extra,
    )(*args)


def shape(dims, kind):
    return jax.ShapeDtypeStruct(dims, kind)


def user_kernel(me_ref, user_hbm, spread_ref, positive_ref, half_ref, own_ref, sems):
    core = lax.rem(me_ref[0], NC)
    half = pl.ds(pl.multiple_of(core * HALF, HALF), HALF)
    own = pl.ds(pl.multiple_of(me_ref[0] * ITEMS, ITEMS), ITEMS)
    half_copy = pltpu.make_async_copy(user_hbm.at[half], half_ref, sems.at[0])
    own_copy = pltpu.make_async_copy(user_hbm.at[own], own_ref, sems.at[1])
    half_copy.start()
    own_copy.start()
    half_copy.wait()
    unit = unit_rows(half_ref[...].astype(f32)).astype(bf16)
    for peer in range(NY):
        spread_ref[peer] = unit
    own_copy.wait()
    positive_ref[...] = unit_rows(own_ref[...].astype(f32)).astype(bf16)


def tower_kernel(
    me_ref,
    emb_ref,
    w_one_ref,
    w_two_ref,
    owner_ref,
    slot_ref,
    spread_ref,
    dir_ref,
    scale_ref,
    base_ref,
    pick_ref,
):
    emb = emb_ref[...]
    pair = lax.broadcasted_iota(jnp.int32, (2, META), 0)
    lane = lax.broadcasted_iota(jnp.int32, (2, META), 1)
    at_owner = jnp.where(lane == 2 * pair, 1.0, 0.0)
    at_slot = jnp.where(lane == 2 * pair + 1, 1.0, 0.0)
    meta = tn(owner_ref[...].astype(f32), at_owner) + tn(slot_ref[...].astype(f32), at_slot)
    base_ref[:, :EMB] = emb
    base_ref[:, EMB:] = meta.astype(bf16)
    preact = nn(emb, w_one_ref[...])
    hidden = (preact * jax.nn.sigmoid(preact)).astype(bf16)
    item_out = nn(hidden, w_two_ref[...])
    scale = lax.rsqrt(jnp.sum(item_out * item_out, axis=1, keepdims=True) + epsilon)
    item_dir = item_out * scale
    unit = item_dir.astype(bf16)
    for peer in range(NZ):
        spread_ref[peer] = unit
    dir_ref[...] = item_dir
    scale_ref[...] = jnp.broadcast_to(scale, (ITEMS, 128))
    count = H // (NX * NC)
    hidden_unit = lax.broadcasted_iota(jnp.int32, (H, count), 0)
    column = lax.broadcasted_iota(jnp.int32, (H, count), 1)
    chosen = hidden_unit == column * (NX * NC) + me_ref[0]
    pick_ref[...] = jnp.where(chosen, 1.0, 0.0).astype(bf16)


def score_kernel(items_ref, own_ref, other_ref, powers_ref, sums_ref):
    items = items_ref[...]
    for step in range(USERS // SCORE_BLOCK):
        users_ref = own_ref if step < USERS // SCORE_BLOCK // 2 else other_ref
        first = step * SCORE_BLOCK % (USERS // 2)
        exponents = nt(items, users_ref[first : first + SCORE_BLOCK, :]) * score_exponent
        powers = jnp.exp2(exponents)
        first = step * SCORE_BLOCK
        powers_ref[:, first : first + SCORE_BLOCK] = powers.astype(bf16)
        sums = jnp.sum(powers, axis=0, keepdims=True)
        for k in range(SCORE_BLOCK // 128):
            row = first // 128 + k
            sums_ref[row : row + 1, :] = sums[:, k * 128 : (k + 1) * 128]


def pair_kernel(mine_ref, theirs_ref, spread_ref):
    half = USERS // 128 // 2
    theirs = theirs_ref[...]
    total = mine_ref[...] + jnp.concatenate([theirs[half:], theirs[:half]], axis=0)
    spread_ref[...] = jnp.broadcast_to(total.astype(bf16)[None], spread_ref.shape)


def unit_cot_kernel(parts_ref, own_ref, other_ref, powers_ref, out_ref, scaled_ref):
    half = USERS // 128 // 2
    totals = parts_ref[0].astype(f32)
    for peer in range(1, NY * NX):
        totals += parts_ref[peer].astype(f32)
    inverse = jnp.transpose(1.0 / totals)
    for k in range(USERS // 128):
        users_ref = own_ref if k < half else other_ref
        first = k % half * 128
        block = users_ref[first : first + 128, :].astype(f32) * inverse[:, k : k + 1]
        scaled_ref[k * 128 : (k + 1) * 128, :] = block.astype(bf16)
    out_ref[...] = nn(powers_ref[...], scaled_ref[...]).astype(bf16)


def cot_kernel(parts_ref, positive_ref, dir_ref, scale_ref, base_ref, spread_ref):
    unit_cot = parts_ref[0].astype(f32)
    for peer in range(1, NZ):
        unit_cot += parts_ref[peer].astype(f32)
    unit_cot -= positive_ref[...].astype(f32)
    item_dir = dir_ref[...]
    along = jnp.sum(item_dir * unit_cot, axis=1, keepdims=True)
    out_cot = ((unit_cot - item_dir * along) * scale_ref[:, :1]).astype(bf16)
    base = base_ref[...]
    for peer in range(NX):
        spread_ref[peer, :, : EMB + META] = base
        spread_ref[peer, :, EMB + META :] = out_cot


def grads_kernel(me_ref, fact_ref, w_one_ref, w_two_ref, pick_ref, table_ref, part_ref):
    me = me_ref[0]
    emb = fact_ref[:, :EMB]
    meta = fact_ref[:, EMB : EMB + META].astype(f32)
    cot = fact_ref[:, EMB + META :]
    w_one = w_one_ref[...]
    preact = nn(emb, w_one)
    sig = jax.nn.sigmoid(preact)
    hidden = (preact * sig).astype(bf16)
    slopes = sig * (1.0 + preact * (1.0 - sig))
    preact_cot = (nt(cot, w_two_ref[...]) * slopes).astype(bf16)
    emb_cot = nt(preact_cot, w_one)
    mine = me.astype(f32)
    slots = lax.broadcasted_iota(jnp.int32, (GROUP, TOUCH), 1).astype(f32)
    placing = jnp.where((meta[:, 0:1] == mine) & (meta[:, 1:2] == slots), 1.0, 0.0)
    placing += jnp.where((meta[:, 2:3] == mine) & (meta[:, 3:4] == slots), 1.0, 0.0)
    table_ref[...] = tn(placing.astype(bf16), emb_cot.astype(bf16))
    pick = pick_ref[...]
    part_ref[:, 0, :] = tn(nn(preact_cot, pick).astype(bf16), emb).astype(bf16)
    part_ref[:, 1, :] = tn(nn(hidden, pick).astype(bf16), cot).astype(bf16)


def gather_pair(values):
    return lax.all_gather(values, "c", axis=0, tiled=True)


def trade_pair(values):
    return lax.ppermute(values, "c", [(0, 1), (1, 0)])


def on_device(user_vec, item_emb, w_one, w_two, item_owner, item_slot):
    me = lax.axis_index("x") * NC + lax.axis_index("c")
    place = me.reshape(1)
    vmem = pl.BlockSpec(memory_space=pltpu.VMEM)
    smem = pl.BlockSpec(memory_space=pltpu.SMEM)
    hbm = pl.BlockSpec(memory_space=pltpu.HBM)
    user_spread, positive = call(
        user_kernel,
        (shape((NY, HALF, W), bf16), shape((ITEMS, W), bf16)),
        (place, user_vec),
        4 * HALF * W,
        grid=(),
        in_specs=[smem, hbm],
        out_specs=(vmem, vmem),
        scratch=(
            pltpu.VMEM((HALF, W), bf16),
            pltpu.VMEM((ITEMS, W), bf16),
            pltpu.SemaphoreType.DMA((2,)),
        ),
        vmem=LARGE,
    )
    users = lax.all_to_all(user_spread, "y", 0, 0)
    users = users.reshape(NY * HALF, W)
    others = trade_pair(users)
    item_spread, item_dir, item_scale, base, pick = call(
        tower_kernel,
        (
            shape((NZ, ITEMS, W), bf16),
            shape((ITEMS, W), f32),
            shape((ITEMS, 128), f32),
            shape((ITEMS, EMB + META), bf16),
            shape((H, H // (NX * NC)), bf16),
        ),
        (place, item_emb, w_one, w_two, item_owner.T, item_slot.T),
        4 * ITEMS * EMB * H,
        grid=(),
        in_specs=[smem, vmem, vmem, vmem, vmem, vmem],
        out_specs=(vmem,) * 5,
    )
    count = NZ * ITEMS
    items = lax.all_to_all(item_spread, "z", 0, 0).reshape(count, W)
    powers, sums = call(
        score_kernel,
        (shape((count, USERS), bf16), shape((USERS // 128, 128), f32)),
        (items, users, others),
        2 * count * USERS * W,
        exps=count * USERS,
    )
    sums = call(
        pair_kernel,
        (shape((NY * NX, USERS // 128, 128), bf16),),
        (sums, trade_pair(sums)),
        USERS,
    )[0]
    sums = lax.all_to_all(sums, ("y", "x"), 0, 0)
    partial = call(
        unit_cot_kernel,
        (shape((count, W), bf16),),
        (sums, users, others, powers),
        2 * count * USERS * W,
        scratch=(pltpu.VMEM((USERS, W), bf16),),
    )[0]
    parts = lax.all_to_all(partial.reshape(NZ, ITEMS, W), "z", 0, 0)
    facts = call(
        cot_kernel,
        (shape((NX, ITEMS, FACT), bf16),),
        (parts, positive, item_dir, item_scale, base),
        NZ * ITEMS * W,
    )[0]
    facts = gather_pair(lax.all_to_all(facts, "x", 0, 0).reshape(NX * ITEMS, FACT))
    table_grad, part = call(
        grads_kernel,
        (shape((TOUCH, EMB), f32), shape((H // (NX * NC), 2, W), bf16)),
        (place, facts, w_one, w_two, pick),
        2 * GROUP * EMB * H * 5,
        grid=(),
        in_specs=[smem, vmem, vmem, vmem, vmem],
        out_specs=(vmem, vmem),
    )
    part = lax.all_to_all(part, ("z", "y"), 0, 0, tiled=True)
    w_grads = jnp.sum(part.astype(f32), axis=0).reshape(1, EMB + W)
    return (table_grad, w_grads)


def solution(mesh):
    fine = Mesh(mesh.devices.reshape(NZ, NY, NX, NC), ("z", "y", "x", "c"))
    dp, every = ("z", "y"), ("z", "y", "x", "c")
    placed = (P(dp, None), P(every, None), P(), P(), P(every, None), P(every, None))
    return jax.shard_map(
        on_device,
        mesh=fine,
        in_specs=placed,
        out_specs=(P(every, None), P(every, None)),
        check_vma=False,
    )
```

```python
import jax
import jax.numpy as jnp
from jax import lax
from jax.experimental import pallas as pl
from jax.experimental.pallas import tpu as pltpu
from jax.sharding import Mesh, PartitionSpec as P

TOUCH = 64
NZ, NY, NX, NC = 16, 8, 4, 2
ITEMS = 32
EMB = 256
W = 256
H = 1024
GROUP = ITEMS * NX * NC
HALF = GROUP // NC
USERS = NY * GROUP
SCORE_BLOCK = 256
LARGE = 63 * 1024 * 1024 + 512 * 1024
META = 128
FACT = EMB + W + META

score_exponent = 1.4426950408889634 / 0.02
epsilon = 1e-06
f32, bf16 = jnp.float32, jnp.bfloat16


def nn(left, right):
    return lax.dot_general(left, right, (((1,), (0,)), ((), ())), preferred_element_type=f32)


def nt(left, right):
    return lax.dot_general(left, right, (((1,), (1,)), ((), ())), preferred_element_type=f32)


def tn(left, right):
    return lax.dot_general(left, right, (((0,), (0,)), ((), ())), preferred_element_type=f32)


def unit_rows(values):
    return values * lax.rsqrt(jnp.sum(values * values, axis=-1, keepdims=True) + epsilon)


def call(body, outs, args, flops, grid=None, in_specs=None, out_specs=None, scratch=(), exps=0, vmem=24 * 1024 * 1024):
    moved = sum(a.size * a.dtype.itemsize for a in args)
    moved += sum(o.size * o.dtype.itemsize for o in outs)
    extra = {} if grid is None else dict(grid=grid, in_specs=in_specs, out_specs=out_specs)
    return pl.pallas_call(
        body,
        out_shape=outs,
        scratch_shapes=list(scratch),
        cost_estimate=pl.CostEstimate(flops=flops, bytes_accessed=moved, transcendentals=exps),
        compiler_params=pltpu.CompilerParams(vmem_limit_bytes=vmem),
        **extra,
    )(*args)


def shape(dims, kind):
    return jax.ShapeDtypeStruct(dims, kind)


def user_kernel(me_ref, user_hbm, spread_ref, positive_ref, half_ref, own_ref, sems):
    core = lax.rem(me_ref[0], NC)
    half = pl.ds(pl.multiple_of(core * HALF, HALF), HALF)
    own = pl.ds(pl.multiple_of(me_ref[0] * ITEMS, ITEMS), ITEMS)
    half_copy = pltpu.make_async_copy(user_hbm.at[half], half_ref, sems.at[0])
    own_copy = pltpu.make_async_copy(user_hbm.at[own], own_ref, sems.at[1])
    half_copy.start()
    own_copy.start()
    half_copy.wait()
    unit = unit_rows(half_ref[...].astype(f32)).astype(bf16)
    for peer in range(NY):
        spread_ref[peer] = unit
    own_copy.wait()
    positive_ref[...] = unit_rows(own_ref[...].astype(f32)).astype(bf16)


def tower_kernel(
    me_ref,
    emb_ref,
    w_one_ref,
    w_two_ref,
    owner_ref,
    slot_ref,
    spread_ref,
    dir_ref,
    scale_ref,
    base_ref,
    pick_ref,
):
    emb = emb_ref[...]
    pair = lax.broadcasted_iota(jnp.int32, (2, META), 0)
    lane = lax.broadcasted_iota(jnp.int32, (2, META), 1)
    at_owner = jnp.where(lane == 2 * pair, 1.0, 0.0)
    at_slot = jnp.where(lane == 2 * pair + 1, 1.0, 0.0)
    meta = tn(owner_ref[...].astype(f32), at_owner) + tn(slot_ref[...].astype(f32), at_slot)
    base_ref[:, :EMB] = emb
    base_ref[:, EMB:] = meta.astype(bf16)
    preact = nn(emb, w_one_ref[...])
    hidden = (preact * jax.nn.sigmoid(preact)).astype(bf16)
    item_out = nn(hidden, w_two_ref[...])
    scale = lax.rsqrt(jnp.sum(item_out * item_out, axis=1, keepdims=True) + epsilon)
    item_dir = item_out * scale
    unit = item_dir.astype(bf16)
    for peer in range(NZ):
        spread_ref[peer] = unit
    dir_ref[...] = item_dir
    scale_ref[...] = jnp.broadcast_to(scale, (ITEMS, 128))
    count = H // (NX * NC)
    hidden_unit = lax.broadcasted_iota(jnp.int32, (H, count), 0)
    column = lax.broadcasted_iota(jnp.int32, (H, count), 1)
    chosen = hidden_unit == column * (NX * NC) + me_ref[0]
    pick_ref[...] = jnp.where(chosen, 1.0, 0.0).astype(bf16)


def score_kernel(items_ref, own_ref, other_ref, powers_ref, sums_ref):
    items = items_ref[...]
    for step in range(USERS // SCORE_BLOCK):
        users_ref = own_ref if step < USERS // SCORE_BLOCK // 2 else other_ref
        first = step * SCORE_BLOCK % (USERS // 2)
        exponents = nt(items, users_ref[first : first + SCORE_BLOCK, :]) * score_exponent
        powers = jnp.exp2(exponents)
        first = step * SCORE_BLOCK
        powers_ref[:, first : first + SCORE_BLOCK] = powers.astype(bf16)
        sums = jnp.sum(powers, axis=0, keepdims=True)
        for k in range(SCORE_BLOCK // 128):
            row = first // 128 + k
            sums_ref[row : row + 1, :] = sums[:, k * 128 : (k + 1) * 128]


def pair_kernel(mine_ref, theirs_ref, spread_ref):
    half = USERS // 128 // 2
    theirs = theirs_ref[...]
    total = mine_ref[...] + jnp.concatenate([theirs[half:], theirs[:half]], axis=0)
    spread_ref[...] = jnp.broadcast_to(total.astype(bf16)[None], spread_ref.shape)


def unit_cot_kernel(parts_ref, own_ref, other_ref, powers_ref, out_ref):
    half = USERS // 128 // 2
    totals = parts_ref[0].astype(f32)
    for peer in range(1, NY * NX):
        totals += parts_ref[peer].astype(f32)
    inverse = jnp.transpose(1.0 / totals)
    total = None
    for first in range(0, USERS, 512):
        scaled = []
        for k in range(first // 128, first // 128 + 4):
            users_ref = own_ref if k < half else other_ref
            rows = slice(k % half * 128, k % half * 128 + 128)
            scaled.append((users_ref[rows, :].astype(f32) * inverse[:, k : k + 1]).astype(bf16))
        product = nn(powers_ref[:, first : first + 512], jnp.concatenate(scaled, axis=0))
        total = product if total is None else total + product
    out_ref[...] = total.astype(bf16)


def cot_kernel(parts_ref, positive_ref, dir_ref, scale_ref, base_ref, spread_ref):
    unit_cot = parts_ref[0].astype(f32)
    for peer in range(1, NZ):
        unit_cot += parts_ref[peer].astype(f32)
    unit_cot -= positive_ref[...].astype(f32)
    item_dir = dir_ref[...]
    along = jnp.sum(item_dir * unit_cot, axis=1, keepdims=True)
    out_cot = ((unit_cot - item_dir * along) * scale_ref[:, :1]).astype(bf16)
    base = base_ref[...]
    for peer in range(NX):
        spread_ref[peer, :, : EMB + META] = base
        spread_ref[peer, :, EMB + META :] = out_cot


def grads_kernel(me_ref, fact_ref, w_one_ref, w_two_ref, pick_ref, table_ref, part_ref):
    me = me_ref[0]
    emb = fact_ref[:, :EMB]
    meta = fact_ref[:, EMB : EMB + META].astype(f32)
    cot = fact_ref[:, EMB + META :]
    w_one = w_one_ref[...]
    preact = nn(emb, w_one)
    sig = jax.nn.sigmoid(preact)
    hidden = (preact * sig).astype(bf16)
    slopes = sig * (1.0 + preact * (1.0 - sig))
    preact_cot = (nt(cot, w_two_ref[...]) * slopes).astype(bf16)
    emb_cot = nt(preact_cot, w_one)
    mine = me.astype(f32)
    slots = lax.broadcasted_iota(jnp.int32, (GROUP, TOUCH), 1).astype(f32)
    placing = jnp.where((meta[:, 0:1] == mine) & (meta[:, 1:2] == slots), 1.0, 0.0)
    placing += jnp.where((meta[:, 2:3] == mine) & (meta[:, 3:4] == slots), 1.0, 0.0)
    table_ref[...] = tn(placing.astype(bf16), emb_cot.astype(bf16))
    pick = pick_ref[...]
    part_ref[:, 0, :] = tn(nn(preact_cot, pick).astype(bf16), emb).astype(bf16)
    part_ref[:, 1, :] = tn(nn(hidden, pick).astype(bf16), cot).astype(bf16)


def gather_pair(values):
    return lax.all_gather(values, "c", axis=0, tiled=True)


def trade_pair(values):
    return lax.ppermute(values, "c", [(0, 1), (1, 0)])


def on_device(user_vec, item_emb, w_one, w_two, item_owner, item_slot):
    me = lax.axis_index("x") * NC + lax.axis_index("c")
    place = me.reshape(1)
    vmem = pl.BlockSpec(memory_space=pltpu.VMEM)
    smem = pl.BlockSpec(memory_space=pltpu.SMEM)
    hbm = pl.BlockSpec(memory_space=pltpu.HBM)
    user_spread, positive = call(
        user_kernel,
        (shape((NY, HALF, W), bf16), shape((ITEMS, W), bf16)),
        (place, user_vec),
        4 * HALF * W,
        grid=(),
        in_specs=[smem, hbm],
        out_specs=(vmem, vmem),
        scratch=(
            pltpu.VMEM((HALF, W), bf16),
            pltpu.VMEM((ITEMS, W), bf16),
            pltpu.SemaphoreType.DMA((2,)),
        ),
        vmem=LARGE,
    )
    users = lax.all_to_all(user_spread, "y", 0, 0)
    users = users.reshape(NY * HALF, W)
    others = trade_pair(users)
    item_spread, item_dir, item_scale, base, pick = call(
        tower_kernel,
        (
            shape((NZ, ITEMS, W), bf16),
            shape((ITEMS, W), f32),
            shape((ITEMS, 128), f32),
            shape((ITEMS, EMB + META), bf16),
            shape((H, H // (NX * NC)), bf16),
        ),
        (place, item_emb, w_one, w_two, item_owner.T, item_slot.T),
        4 * ITEMS * EMB * H,
        grid=(),
        in_specs=[smem, vmem, vmem, vmem, vmem, vmem],
        out_specs=(vmem,) * 5,
    )
    count = NZ * ITEMS
    items = lax.all_to_all(item_spread, "z", 0, 0).reshape(count, W)
    powers, sums = call(
        score_kernel,
        (shape((count, USERS), bf16), shape((USERS // 128, 128), f32)),
        (items, users, others),
        2 * count * USERS * W,
        exps=count * USERS,
    )
    sums = call(
        pair_kernel,
        (shape((NY * NX, USERS // 128, 128), bf16),),
        (sums, trade_pair(sums)),
        USERS,
    )[0]
    sums = lax.all_to_all(sums, ("y", "x"), 0, 0)
    partial = call(
        unit_cot_kernel,
        (shape((count, W), bf16),),
        (sums, users, others, powers),
        2 * count * USERS * W,
    )[0]
    parts = lax.all_to_all(partial.reshape(NZ, ITEMS, W), "z", 0, 0)
    facts = call(
        cot_kernel,
        (shape((NX, ITEMS, FACT), bf16),),
        (parts, positive, item_dir, item_scale, base),
        NZ * ITEMS * W,
    )[0]
    facts = gather_pair(lax.all_to_all(facts, "x", 0, 0).reshape(NX * ITEMS, FACT))
    table_grad, part = call(
        grads_kernel,
        (shape((TOUCH, EMB), f32), shape((H // (NX * NC), 2, W), bf16)),
        (place, facts, w_one, w_two, pick),
        2 * GROUP * EMB * H * 5,
        grid=(),
        in_specs=[smem, vmem, vmem, vmem, vmem],
        out_specs=(vmem, vmem),
    )
    part = lax.all_to_all(part, ("z", "y"), 0, 0, tiled=True)
    w_grads = jnp.sum(part.astype(f32), axis=0).reshape(1, EMB + W)
    return (table_grad, w_grads)


def solution(mesh):
    fine = Mesh(mesh.devices.reshape(NZ, NY, NX, NC), ("z", "y", "x", "c"))
    dp, every = ("z", "y"), ("z", "y", "x", "c")
    placed = (P(dp, None), P(every, None), P(), P(), P(every, None), P(every, None))
    return jax.shard_map(
        on_device,
        mesh=fine,
        in_specs=placed,
        out_specs=(P(every, None), P(every, None)),
        check_vma=False,
    )
```
